32 devices in a mesh: patch: 8 (over y, x, core), tensor: 4 (over z).
Axes of the slice: x: 2, y: 2, z: 4, core: 2. Of those that a mesh axis runs over, the one named last changes fastest.
Arguments:
- query: bfloat16 [4096, 5120], P('patch', 'tensor'), may hold values from -6 to 6
- key_fresh: bfloat16 [4096, 5120], P('patch', 'tensor'), may hold values from -6 to 6
- value_fresh: bfloat16 [4096, 5120], P('patch', 'tensor'), may hold values from -6 to 6
- key_stale: bfloat16 [4096, 5120], P('patch', 'tensor'), may hold values from -6 to 6
- value_stale: bfloat16 [4096, 5120], P('patch', 'tensor'), may hold values from -6 to 6
- out_weight: bfloat16 [5120, 5120], P('tensor'), may hold values from -0.078125 to 0.078125
- residual: bfloat16 [4096, 5120], P('patch', 'tensor'), may hold values from -6 to 6
- gate: float32 [5120], P('tensor'), may hold values from 0.5 to 1.5
Outputs:
- block_out: bfloat16 [4096, 5120], P('patch', 'tensor')
The draws below stay inside these ranges and needn't reach their ends.
All inputs are finite; a program needn't handle non-finite values.
Results may differ from the reference program's by a relative error of at most 0.006.
Values may be sent and summed in bfloat16 or wider, within the bound.
A program may use at most 128 MiB of HBM per device.

```python
import jax
import jax.numpy as jnp
from jax import lax

D = 5120
HEADS = 40
HD = 128
TOK_DEV = 512
TOKENS = 4096
HEADS_DEV = 10
N_PATCH = 8
N_TENSOR = 4


def draw_query(key, part):
    own_key = jax.random.fold_in(key, 1)
    values = jnp.clip(1.3 * jax.random.normal(own_key, (TOKENS, HEADS * HD), jnp.float32), -6.0, 6.0)
    return values.astype(jnp.bfloat16)


def draw_key_stale(key, part):
    own_key = jax.random.fold_in(key, 2)
    values = jnp.clip(1.3 * jax.random.normal(own_key, (TOKENS, HEADS * HD), jnp.float32), -6.0, 6.0)
    return values.astype(jnp.bfloat16)


def levels(key, dims, split, least, high):
    level, own = 1.0, jax.random.fold_in(key, 6)
    for dim, shards_of in split:
        heights = jnp.exp(jax.random.uniform(jax.random.fold_in(own, dim), (shards_of,), jnp.float32, least / len(split), high / len(split)))
        level = level * jnp.repeat(heights, dims[dim] // shards_of).reshape([-1 if axis == dim else 1 for axis in range(len(dims))])
    return level


def centred(stream_key, shape, scale, limit, split=(), held_as=jnp.bfloat16):
    factor_of = levels(stream_key, shape, split, -0.22, 0.18) if split else 1.0
    values = jax.random.normal(stream_key, shape, jnp.float32) * scale * factor_of
    return jnp.minimum(jnp.maximum(values, -limit), limit).astype(held_as)


def setup_inputs(seed: int = 0) -> dict:
    streams_of = jax.random.split(jax.random.key(seed), 9)
    query = draw_query(jax.random.fold_in(streams_of[8], 71), 0)
    key_fresh = centred(streams_of[1], (TOKENS, HEADS * HD), 1.3, 6.0, ((0, 8), (1, 4)))
    value_fresh = centred(streams_of[2], (TOKENS, HEADS * HD), 1.0, 6.0, ((0, 8), (1, 4)))
    key_stale = draw_key_stale(jax.random.fold_in(streams_of[8], 71), 0)
    value_stale = centred(streams_of[4], (TOKENS, HEADS * HD), 1.0, 6.0, ((0, 8), (1, 4)))
    out_weight = centred(streams_of[5], (HEADS * HD, D), (HEADS * HD) ** -0.5, 0.078125, ((0, 4),))
    residual = centred(streams_of[6], (TOKENS, D), 1.0, 6.0, ((0, 8), (1, 4)))
    gate = jnp.clip(1.0 + 0.1 * jax.random.normal(streams_of[7], (D,), jnp.float32), 0.5, 1.5)
    return {"query": query, "key_fresh": key_fresh, "value_fresh": value_fresh, "key_stale": key_stale, "value_stale": value_stale, "out_weight": out_weight, "residual": residual, "gate": gate}


def reference(query, key_fresh, value_fresh, key_stale, value_stale, out_weight, residual, gate):
    scale = HD ** -0.5

    def heads_first(array):
        return array.reshape(TOKENS, HEADS, HD).transpose(1, 0, 2)

    def one_head(pieces):
        q_head, k_new, v_new, k_old, v_old = pieces

        def one_block(block):
            start = (block * TOK_DEV).astype(jnp.int32)
            q_rows = lax.dynamic_slice_in_dim(q_head, start, TOK_DEV, 0)
            keys = lax.dynamic_update_slice_in_dim(k_old, lax.dynamic_slice_in_dim(k_new, start, TOK_DEV, 0), start, 0)
            values = lax.dynamic_update_slice_in_dim(v_old, lax.dynamic_slice_in_dim(v_new, start, TOK_DEV, 0), start, 0)
            scores = jnp.dot(q_rows, keys.T, preferred_element_type=jnp.float32) * scale
            expo = jnp.exp(scores - jnp.max(scores, axis=-1, keepdims=True))
            total = jnp.sum(expo, axis=-1, keepdims=True)
            mixed = jnp.dot(expo.astype(jnp.bfloat16), values, preferred_element_type=jnp.float32)
            return (mixed / total).astype(jnp.bfloat16)

        return lax.map(one_block, jnp.arange(N_PATCH, dtype=jnp.int32)).reshape(TOKENS, HD)

    stacked = lax.map(one_head, (heads_first(query), heads_first(key_fresh), heads_first(value_fresh), heads_first(key_stale), heads_first(value_stale)))
    attended = stacked.transpose(1, 0, 2).reshape(TOKENS, HEADS * HD)
    group = HEADS_DEV * HD

    def add_group(running, index):
        first = (index * group).astype(jnp.int32)
        part = jnp.dot(lax.dynamic_slice_in_dim(attended, first, group, 1), lax.dynamic_slice_in_dim(out_weight, first, group, 0), preferred_element_type=jnp.float32)
        rounded = lax.optimization_barrier(part.astype(jnp.bfloat16))
        return running + rounded.astype(jnp.float32), None

    projected, _ = lax.scan(add_group, jnp.zeros((TOKENS, D), jnp.float32), jnp.arange(N_TENSOR, dtype=jnp.int32))
    return (residual.astype(jnp.float32) + gate.astype(jnp.float32)[None, :] * projected).astype(jnp.bfloat16)
```

```python
import functools
import math

import jax
import jax.numpy as jnp
from jax import lax
from jax.experimental import pallas as pl
from jax.experimental.pallas import tpu as pltpu
from jax.sharding import PartitionSpec as P

HD = 128
SCALE = HD ** -0.5 * math.log2(math.e)


def attend_block(q, k, v, m_old, acc_old):
    s = lax.dot_general(q, k, (((1,), (1,)), ((), ())), preferred_element_type=jnp.float32) * SCALE
    m_new = jnp.maximum(m_old, jnp.max(s, axis=-1, keepdims=True))
    p = jnp.exp2(s - m_new).astype(jnp.bfloat16)
    v1 = jnp.concatenate([v, jnp.ones_like(v)], axis=1)
    add = jnp.dot(p, v1, preferred_element_type=jnp.float32)
    return m_new, acc_old * jnp.exp2(m_old - m_new) + add


def flash_kernel(n, q_ref, kf_ref, vf_ref, ks_ref, vs_ref, o_ref):
    rows = q_ref.shape[0]
    own = lax.axis_index("patch")
    q = q_ref[...]
    m0 = jnp.full((rows, 1), -1e30, jnp.float32)
    a0 = jnp.zeros((rows, 2 * HD), jnp.float32)
    state = attend_block(q, kf_ref[...], vf_ref[...], m0, a0)

    def inner(j, state):
        first = pl.multiple_of(lax.rem(own + j, n) * rows, rows)
        return attend_block(q, ks_ref[pl.ds(first, rows), :], vs_ref[pl.ds(first, rows), :], *state)

    m, acc = lax.fori_loop(1, n, inner, state)
    o_ref[...] = (acc[:, :HD] / acc[:, HD:]).astype(o_ref.dtype)


def general_body(n, query, key_fresh, value_fresh, key_stale, value_stale, out_weight, residual, gate):
    rows, cols = query.shape
    keys = lax.all_gather(key_stale, "patch", axis=0, tiled=True)
    values = lax.all_gather(value_stale, "patch", axis=0, tiled=True)
    local = pl.BlockSpec((rows, HD), lambda h: (0, h))
    whole = pl.BlockSpec((rows * n, HD), lambda h: (0, h))
    attended = pl.pallas_call(
        functools.partial(flash_kernel, n),
        grid=(cols // HD,),
        in_specs=[local, local, local, whole, whole],
        out_specs=local,
        out_shape=jax.ShapeDtypeStruct((rows, cols), jnp.bfloat16),
        compiler_params=pltpu.CompilerParams(vmem_limit_bytes=48 * 2**20),
        name="flash",
    )(query, key_fresh, value_fresh, keys, values)
    partial = jnp.dot(attended, out_weight, preferred_element_type=jnp.float32).astype(jnp.bfloat16)
    mine = lax.psum_scatter(partial, "tensor", scatter_dimension=1, tiled=True).astype(jnp.float32)
    return (residual.astype(jnp.float32) + gate[None, :] * mine).astype(jnp.bfloat16)


def solution(mesh):
    n = mesh.shape["patch"]
    both = P("patch", "tensor")
    return jax.shard_map(
        functools.partial(general_body, n),
        mesh=mesh,
        in_specs=(both,) * 5 + (P("tensor", None), both, P("tensor")),
        out_specs=both,
        check_vma=False,
    )
```

```python
import functools
import math

import jax
import jax.numpy as jnp
from jax import lax
from jax.experimental import pallas as pl
from jax.experimental.pallas import tpu as pltpu
from jax.sharding import PartitionSpec as P

HD = 128
SCALE = HD ** -0.5 * math.log2(math.e)


def attend_block(q, k, v, m_old, acc_old):
    s = lax.dot_general(q, k, (((1,), (1,)), ((), ())), preferred_element_type=jnp.float32) * SCALE
    m_new = jnp.maximum(m_old, jnp.max(s, axis=-1, keepdims=True))
    p = jnp.exp2(s - m_new).astype(jnp.bfloat16)
    v1 = jnp.concatenate([v, jnp.ones_like(v)], axis=1)
    add = jnp.dot(p, v1, preferred_element_type=jnp.float32)
    return m_new, acc_old * jnp.exp2(m_old - m_new) + add


def flash_kernel(n, q_ref, kf_ref, vf_ref, ks_ref, vs_ref, o_ref):
    rows = q_ref.shape[0]
    own = lax.axis_index("patch")
    q = q_ref[...]
    m0 = jnp.full((rows, 1), -1e30, jnp.float32)
    a0 = jnp.zeros((rows, 2 * HD), jnp.float32)
    state = attend_block(q, kf_ref[...], vf_ref[...], m0, a0)

    def inner(j, state):
        first = pl.multiple_of(lax.rem(own + j, n) * rows, rows)
        return attend_block(q, ks_ref[pl.ds(first, rows), :], vs_ref[pl.ds(first, rows), :], *state)

    m, acc = lax.fori_loop(1, n, inner, state)
    o_ref[...] = (acc[:, :HD] / acc[:, HD:]).astype(o_ref.dtype)


MESH = pl.DeviceIdType.MESH


def attend_kernel(q_ref, kf_ref, vf_ref, ks_ref, vs_ref, o_ref, kv, qx, osend, orecv, lsend, lrecv,
                  m_s, acc_s, first_s, first_q, fwd_s, ret_s, rec_kv, rec_q, rec_o):
    own = lax.axis_index("patch")
    c, x, y = lax.rem(own, 2), lax.rem(own // 2, 2), own // 4

    def at(ky, kx, kc):
        return lax.rem(y + ky, 2) * 4 + lax.rem(x + kx, 2) * 2 + lax.rem(c + kc, 2)

    pc, px, py, pyx = at(0, 0, 1), at(0, 1, 0), at(1, 0, 0), at(1, 1, 0)
    half = kv.shape[0]
    rows = q_ref.shape[0]

    def head_cols(hx, i):
        return pl.ds(pl.multiple_of((hx * half + i) * HD, HD), HD)

    def send(src, dst, ssem, rsem, dev):
        return pltpu.make_async_remote_copy(src_ref=src, dst_ref=dst, send_sem=ssem, recv_sem=rsem,
                                            device_id={"patch": dev}, device_id_type=MESH)

    def firsts(i):
        mine, theirs = head_cols(x, i), head_cols(1 - x, i)
        out = [send(q_ref.at[:, theirs], qx.at[i], first_q.at[i], rec_q.at[i], px)]
        for t, src in enumerate((ks_ref, vs_ref)):
            out.append(send(src.at[:, theirs], kv.at[i, own, t], first_s.at[0, i, t], rec_kv.at[i, own], px))
            out.append(send(src.at[:, mine], kv.at[i, own, t], first_s.at[1, i, t], rec_kv.at[i, own], py))
            out.append(send(src.at[:, mine], kv.at[i, own, t], first_s.at[2, i, t], rec_kv.at[i, own], pc))
            out.append(pltpu.make_async_copy(src.at[:, mine], kv.at[i, own, t], first_s.at[3, i, t]))
        return out

    def start_first(i):
        for copy in firsts(i):
            copy.start()

    def fwd(kind, i, b, dev):
        return send(kv.at[i, b], kv.at[i, b], fwd_s.at[kind, i], rec_kv.at[i, b], dev)

    def arrived(i, b):
        fwd(0, i, b, pc).wait_recv()

    def back(i):
        return (send(osend.at[i], orecv.at[i], ret_s.at[0, i], rec_o.at[0, i], px),
                send(lsend.at[i], lrecv.at[i], ret_s.at[1, i], rec_o.at[1, i], px))

    def pass_on_x(i):
        arrived(i, px)
        fwd(0, i, px, py).start()
        fwd(1, i, px, pc).start()

    def fold(i, q, blocks):
        for r in range(2):
            m, acc = attend_block(q[r], kv[i, blocks[r], 0], kv[i, blocks[r], 1], m_s[r], acc_s[r])
            m_s[r], acc_s[r] = m, acc

    def merge(i):
        theirs = head_cols(1 - x, i)
        for copy in back(i):
            copy.wait_recv()
        m = jnp.broadcast_to(lrecv[i][0:1, :], (HD, rows)).T[:, 0:1]
        acc = jnp.concatenate([orecv[i].astype(jnp.float32), jnp.ones((rows, HD), jnp.float32)], axis=1)
        m, acc = attend_block(q_ref[:, theirs], kf_ref[:, theirs], vf_ref[:, theirs], m, acc)
        o_ref[:, theirs] = (acc[:, :HD] / acc[:, HD:]).astype(o_ref.dtype)

    barrier = pltpu.get_barrier_semaphore()
    for dev in (pc, px, py):
        pl.semaphore_signal(barrier, inc=1, device_id={"patch": dev}, device_id_type=MESH)
    pl.semaphore_wait(barrier, 3)

    start_first(0)
    start_first(1)

    def one_head(i, _):
        @pl.when(i + 2 < half)
        def _():
            start_first(i + 2)

        mine = head_cols(x, i)
        m0 = jnp.full((rows, 1), -1e30, jnp.float32)
        a0 = jnp.zeros((rows, 2 * HD), jnp.float32)
        m_s[0], acc_s[0] = attend_block(q_ref[:, mine], kf_ref[:, mine], vf_ref[:, mine], m0, a0)
        m_s[1], acc_s[1] = m0, a0

        @pl.when(i == 0)
        def _():
            pass_on_x(0)

        send(q_ref.at[:, mine], qx.at[i], first_q.at[i], rec_q.at[i], px).wait_recv()
        for t, src in enumerate((ks_ref, vs_ref)):
            pltpu.make_async_copy(src.at[:, mine], kv.at[i, own, t], first_s.at[3, i, t]).wait()
        arrived(i, pc)
        arrived(i, at(0, 1, 1))

        def queries():
            return q_ref[:, mine], qx[i]

        def near(t, _):
            kx, kc = (t + 1) // 2, lax.rem(t + 1, 2)
            b0 = at(0, kx, kc)
            b1 = lax.rem(t, 2) * own + (1 - lax.rem(t, 2)) * b0
            fold(i, queries(), (b0, b1))
            return 0

        lax.fori_loop(0, 3, near, 0)

        @pl.when(i + 1 < half)
        def _():
            pass_on_x(i + 1)

        arrived(i, py)
        fwd(2, i, py, pc).start()
        arrived(i, pyx)
        fwd(3, i, pyx, pc).start()

        def far(t, _):
            @pl.when(t == 2)
            def _():
                arrived(i, at(1, 0, 1))
                arrived(i, at(1, 1, 1))

            b = at(1, lax.rem(t, 2), t // 2)
            fold(i, queries(), (b, b))
            return 0

        lax.fori_loop(0, 4, far, 0)
        o_ref[:, mine] = (acc_s[0][:, :HD] / acc_s[0][:, HD:]).astype(o_ref.dtype)
        total = acc_s[1][:, HD:]
        osend[i] = (acc_s[1][:, :HD] / total).astype(osend.dtype)
        lsend[i] = (m_s[1] + jnp.log2(total)).T[0:8, :]
        for copy in back(i):
            copy.start()

        @pl.when(i > 0)
        def _():
            merge(i - 1)

        return 0

    lax.fori_loop(0, half, one_head, 0)
    merge(half - 1)

    def finish(i, _):
        firsts_i = firsts(i)
        firsts_i[0].wait_send()
        for t in range(2):
            for k in range(3):
                firsts_i[1 + 4 * t + k].wait_send()
        for kind, (b, dev) in enumerate(((px, py), (px, pc), (py, pc), (pyx, pc))):
            fwd(kind, i, b, dev).wait_send()
        for copy in back(i):
            copy.wait_send()
        return 0

    lax.fori_loop(0, half, finish, 0)


def paired_attention(query, key_fresh, value_fresh, key_stale, value_stale):
    rows, cols = query.shape
    half = cols // HD // 2
    vmem = pl.BlockSpec(memory_space=pltpu.VMEM)
    hbm = pl.BlockSpec(memory_space=pl.ANY)
    dma = pltpu.SemaphoreType.DMA
    bf16, f32 = jnp.bfloat16, jnp.float32
    return pl.pallas_call(
        attend_kernel,
        in_specs=[vmem, vmem, vmem, hbm, hbm],
        out_specs=vmem,
        out_shape=jax.ShapeDtypeStruct((rows, cols), bf16),
        scratch_shapes=[
            pltpu.VMEM((half, 8, 2, rows, HD), bf16),
            pltpu.VMEM((half, rows, HD), bf16),
            pltpu.VMEM((half, rows, HD), bf16),
            pltpu.VMEM((half, rows, HD), bf16),
            pltpu.VMEM((half, 8, rows), f32),
            pltpu.VMEM((half, 8, rows), f32),
            pltpu.VMEM((2, rows, 1), f32),
            pltpu.VMEM((2, rows, 2 * HD), f32),
            dma((4, half, 2)),
            dma((half,)),
            dma((4, half)),
            dma((2, half)),
            dma((half, 8)),
            dma((half,)),
            dma((2, half)),
        ],
        compiler_params=pltpu.CompilerParams(
            collective_id=1, has_side_effects=True, vmem_limit_bytes=56 * 2**20
        ),
        name="paired_attention",
    )(query, key_fresh, value_fresh, key_stale, value_stale)

def general_body(n, query, key_fresh, value_fresh, key_stale, value_stale, out_weight, residual, gate):
    rows, cols = query.shape
    if n == 8 and cols % (2 * HD) == 0:
        attended = paired_attention(query, key_fresh, value_fresh, key_stale, value_stale)
        return project(attended, out_weight, residual, gate)
    keys = lax.all_gather(key_stale, "patch", axis=0, tiled=True)
    values = lax.all_gather(value_stale, "patch", axis=0, tiled=True)
    local = pl.BlockSpec((rows, HD), lambda h: (0, h))
    whole = pl.BlockSpec((rows * n, HD), lambda h: (0, h))
    attended = pl.pallas_call(
        functools.partial(flash_kernel, n),
        grid=(cols // HD,),
        in_specs=[local, local, local, whole, whole],
        out_specs=local,
        out_shape=jax.ShapeDtypeStruct((rows, cols), jnp.bfloat16),
        compiler_params=pltpu.CompilerParams(vmem_limit_bytes=48 * 2**20),
        name="flash",
    )(query, key_fresh, value_fresh, keys, values)
    return project(attended, out_weight, residual, gate)


def project(attended, out_weight, residual, gate):
    partial = jnp.dot(attended, out_weight, preferred_element_type=jnp.float32).astype(jnp.bfloat16)
    mine = lax.psum_scatter(partial, "tensor", scatter_dimension=1, tiled=True).astype(jnp.float32)
    return (residual.astype(jnp.float32) + gate[None, :] * mine).astype(jnp.bfloat16)


def solution(mesh):
    n = mesh.shape["patch"]
    both = P("patch", "tensor")
    return jax.shard_map(
        functools.partial(general_body, n),
        mesh=mesh,
        in_specs=(both,) * 5 + (P("tensor", None), both, P("tensor")),
        out_specs=both,
        check_vma=False,
    )
```

```python
import functools
import math

import jax
import jax.numpy as jnp
from jax import lax
from jax.experimental import pallas as pl
from jax.experimental.pallas import tpu as pltpu
from jax.sharding import PartitionSpec as P

HD = 128
SCALE = HD ** -0.5 * math.log2(math.e)


def attend_block(q, k, v, m_old, acc_old):
    s = lax.dot_general(q, k, (((1,), (1,)), ((), ())), preferred_element_type=jnp.float32) * SCALE
    m_new = jnp.maximum(m_old, jnp.max(s, axis=-1, keepdims=True))
    p = jnp.exp2(s - m_new).astype(jnp.bfloat16)
    v1 = jnp.concatenate([v, jnp.ones_like(v)], axis=1)
    add = jnp.dot(p, v1, preferred_element_type=jnp.float32)
    return m_new, acc_old * jnp.exp2(m_old - m_new) + add


def flash_kernel(n, q_ref, kf_ref, vf_ref, ks_ref, vs_ref, o_ref):
    rows = q_ref.shape[0]
    own = lax.axis_index("patch")
    q = q_ref[...]
    m0 = jnp.full((rows, 1), -1e30, jnp.float32)
    a0 = jnp.zeros((rows, 2 * HD), jnp.float32)
    state = attend_block(q, kf_ref[...], vf_ref[...], m0, a0)

    def inner(j, state):
        first = pl.multiple_of(lax.rem(own + j, n) * rows, rows)
        return attend_block(q, ks_ref[pl.ds(first, rows), :], vs_ref[pl.ds(first, rows), :], *state)

    m, acc = lax.fori_loop(1, n, inner, state)
    o_ref[...] = (acc[:, :HD] / acc[:, HD:]).astype(o_ref.dtype)


MESH = pl.DeviceIdType.MESH


def attend_kernel(q_ref, kf_ref, vf_ref, ks_ref, vs_ref, w_ref, o_ref, wx_ref, kv, qx, osend, orecv, lsend, lrecv,
                  m_s, acc_s, first_s, first_q, fwd_s, ret_s, rec_kv, rec_q, rec_o, w_s, rec_w):
    own = lax.axis_index("patch")
    c, x, y = lax.rem(own, 2), lax.rem(own // 2, 2), own // 4

    def at(ky, kx, kc):
        return lax.rem(y + ky, 2) * 4 + lax.rem(x + kx, 2) * 2 + lax.rem(c + kc, 2)

    pc, px, py, pyx = at(0, 0, 1), at(0, 1, 0), at(1, 0, 0), at(1, 1, 0)
    half = kv.shape[0]
    rows = q_ref.shape[0]
    z = lax.axis_index("tensor")
    mate = z + 1 - 2 * lax.rem(z, 2)
    outer = lax.rem(z, 3) == 0
    width = wx_ref.shape[1]

    def head_cols(hx, i):
        return pl.ds(pl.multiple_of((hx * half + i) * HD, HD), HD)

    def send(src, dst, ssem, rsem, dev):
        return pltpu.make_async_remote_copy(src_ref=src, dst_ref=dst, send_sem=ssem, recv_sem=rsem,
                                            device_id={"patch": dev}, device_id_type=MESH)

    def firsts(i):
        mine, theirs = head_cols(x, i), head_cols(1 - x, i)
        out = [send(q_ref.at[:, theirs], qx.at[i], first_q.at[i], rec_q.at[i], px)]
        for t, src in enumerate((ks_ref, vs_ref)):
            out.append(send(src.at[:, theirs], kv.at[i, own, t], first_s.at[0, i, t], rec_kv.at[i, own], px))
            out.append(send(src.at[:, mine], kv.at[i, own, t], first_s.at[1, i, t], rec_kv.at[i, own], py))
            out.append(send(src.at[:, mine], kv.at[i, own, t], first_s.at[2, i, t], rec_kv.at[i, own], pc))
            out.append(pltpu.make_async_copy(src.at[:, mine], kv.at[i, own, t], first_s.at[3, i, t]))
        return out

    def weight_rows(core, i):
        return pl.ds(pl.multiple_of((core * half + i) * HD, HD), HD)

    def weight_out(i):
        cols = pl.ds(pl.multiple_of((1 - z // 2) * width, HD), width)
        return pltpu.make_async_remote_copy(
            src_ref=w_ref.at[weight_rows(c, i), cols], dst_ref=wx_ref.at[weight_rows(c, i), :],
            send_sem=w_s.at[i], recv_sem=rec_w.at[0, i], device_id={"tensor": mate}, device_id_type=MESH)

    def weight_on(i, core):
        part = wx_ref.at[weight_rows(core, i), :]
        return send(part, part, w_s.at[i], rec_w.at[1, i], pc)

    def weight_pass(i):
        @pl.when(jnp.logical_not(outer))
        def _():
            weight_out(i).wait_recv()
            weight_on(i, c).start()

    def start_first(i):
        for copy in firsts(i):
            copy.start()

        @pl.when(outer)
        def _():
            weight_out(i).start()

    def fwd(kind, i, b, dev):
        return send(kv.at[i, b], kv.at[i, b], fwd_s.at[kind, i], rec_kv.at[i, b], dev)

    def arrived(i, b):
        fwd(0, i, b, pc).wait_recv()

    def back(i):
        return (send(osend.at[i], orecv.at[i], ret_s.at[0, i], rec_o.at[0, i], px),
                send(lsend.at[i], lrecv.at[i], ret_s.at[1, i], rec_o.at[1, i], px))

    def pass_on_x(i):
        arrived(i, px)
        fwd(0, i, px, py).start()
        fwd(1, i, px, pc).start()

    def fold(i, q, blocks):
        for r in range(2):
            m, acc = attend_block(q[r], kv[i, blocks[r], 0], kv[i, blocks[r], 1], m_s[r], acc_s[r])
            m_s[r], acc_s[r] = m, acc

    def merge(i):
        theirs = head_cols(1 - x, i)
        for copy in back(i):
            copy.wait_recv()
        m = jnp.broadcast_to(lrecv[i][0:1, :], (HD, rows)).T[:, 0:1]
        acc = jnp.concatenate([orecv[i].astype(jnp.float32), jnp.ones((rows, HD), jnp.float32)], axis=1)
        m, acc = attend_block(q_ref[:, theirs], kf_ref[:, theirs], vf_ref[:, theirs], m, acc)
        o_ref[:, theirs] = (acc[:, :HD] / acc[:, HD:]).astype(o_ref.dtype)

    barrier = pltpu.get_barrier_semaphore()
    for dev in (pc, px, py):
        pl.semaphore_signal(barrier, inc=1, device_id={"patch": dev}, device_id_type=MESH)
    pl.semaphore_signal(barrier, inc=1, device_id={"tensor": mate}, device_id_type=MESH)
    pl.semaphore_wait(barrier, 4)

    start_first(0)
    start_first(1)

    def one_head(i, _):
        @pl.when(i + 2 < half)
        def _():
            start_first(i + 2)

        mine = head_cols(x, i)
        m0 = jnp.full((rows, 1), -1e30, jnp.float32)
        a0 = jnp.zeros((rows, 2 * HD), jnp.float32)
        m_s[0], acc_s[0] = attend_block(q_ref[:, mine], kf_ref[:, mine], vf_ref[:, mine], m0, a0)
        m_s[1], acc_s[1] = m0, a0

        @pl.when(i == 0)
        def _():
            pass_on_x(0)

        send(q_ref.at[:, mine], qx.at[i], first_q.at[i], rec_q.at[i], px).wait_recv()
        for t, src in enumerate((ks_ref, vs_ref)):
            pltpu.make_async_copy(src.at[:, mine], kv.at[i, own, t], first_s.at[3, i, t]).wait()
        arrived(i, pc)
        arrived(i, at(0, 1, 1))

        def queries():
            return q_ref[:, mine], qx[i]

        def near(t, _):
            kx, kc = (t + 1) // 2, lax.rem(t + 1, 2)
            b0 = at(0, kx, kc)
            b1 = lax.rem(t, 2) * own + (1 - lax.rem(t, 2)) * b0
            fold(i, queries(), (b0, b1))
            return 0

        lax.fori_loop(0, 3, near, 0)

        @pl.when(i + 1 < half)
        def _():
            pass_on_x(i + 1)

        arrived(i, py)
        fwd(2, i, py, pc).start()
        arrived(i, pyx)
        fwd(3, i, pyx, pc).start()

        def far(t, _):
            @pl.when(t == 2)
            def _():
                arrived(i, at(1, 0, 1))
                arrived(i, at(1, 1, 1))

            b = at(1, lax.rem(t, 2), t // 2)
            fold(i, queries(), (b, b))
            return 0

        lax.fori_loop(0, 4, far, 0)
        o_ref[:, mine] = (acc_s[0][:, :HD] / acc_s[0][:, HD:]).astype(o_ref.dtype)
        total = acc_s[1][:, HD:]
        osend[i] = (acc_s[1][:, :HD] / total).astype(osend.dtype)
        lsend[i] = (m_s[1] + jnp.log2(total)).T[0:8, :]
        for copy in back(i):
            copy.start()

        @pl.when(i > 0)
        def _():
            merge(i - 1)
            weight_pass(i - 1)

        return 0

    lax.fori_loop(0, half, one_head, 0)
    merge(half - 1)
    weight_pass(half - 1)

    def finish(i, _):
        @pl.when(outer)
        def _():
            weight_out(i).wait_send()

        @pl.when(jnp.logical_not(outer))
        def _():
            weight_on(i, c).wait_send()
            weight_on(i, 1 - c).wait_recv()

        firsts_i = firsts(i)
        firsts_i[0].wait_send()
        for t in range(2):
            for k in range(3):
                firsts_i[1 + 4 * t + k].wait_send()
        for kind, (b, dev) in enumerate(((px, py), (px, pc), (py, pc), (pyx, pc))):
            fwd(kind, i, b, dev).wait_send()
        for copy in back(i):
            copy.wait_send()
        return 0

    lax.fori_loop(0, half, finish, 0)


def paired_attention(query, key_fresh, value_fresh, key_stale, value_stale, out_weight):
    rows, cols = query.shape
    half = cols // HD // 2
    vmem = pl.BlockSpec(memory_space=pltpu.VMEM)
    hbm = pl.BlockSpec(memory_space=pl.ANY)
    dma = pltpu.SemaphoreType.DMA
    bf16, f32 = jnp.bfloat16, jnp.float32
    return pl.pallas_call(
        attend_kernel,
        in_specs=[vmem, vmem, vmem, hbm, hbm, hbm],
        out_specs=[vmem, hbm],
        out_shape=[jax.ShapeDtypeStruct((rows, cols), bf16),
                   jax.ShapeDtypeStruct((cols, out_weight.shape[1] // 2), bf16)],
        scratch_shapes=[
            pltpu.VMEM((half, 8, 2, rows, HD), bf16),
            pltpu.VMEM((half, rows, HD), bf16),
            pltpu.VMEM((half, rows, HD), bf16),
            pltpu.VMEM((half, rows, HD), bf16),
            pltpu.VMEM((half, 8, rows), f32),
            pltpu.VMEM((half, 8, rows), f32),
            pltpu.VMEM((2, rows, 1), f32),
            pltpu.VMEM((2, rows, 2 * HD), f32),
            dma((4, half, 2)),
            dma((half,)),
            dma((4, half)),
            dma((2, half)),
            dma((half, 8)),
            dma((half,)),
            dma((2, half)),
            dma((half,)),
            dma((2, half)),
        ],
        compiler_params=pltpu.CompilerParams(
            collective_id=1, has_side_effects=True, vmem_limit_bytes=56 * 2**20
        ),
        name="paired_attention",
    )(query, key_fresh, value_fresh, key_stale, value_stale, out_weight)


def project_kernel(a_ref, w_ref, wx_ref, res_ref, gate_ref, o_ref, w, wx, am, pm, sfo, spe, f, tfo, tpe,
                   fs, ps, own_s, w_s, send_s, rec_s):
    z = lax.axis_index("tensor")
    mate = z + 1 - 2 * lax.rem(z, 2)
    outer = lax.rem(z, 3) == 0
    inner = jnp.logical_not(outer)
    peer = 3 - z
    far = 2 * (1 - z // 2)
    jfo, jpe = lax.rem(z, 2), 1 - lax.rem(z, 2)
    chunks, step, share = am.shape

    def load(s):
        cols = pl.ds(pl.multiple_of(s * share, HD), share)
        return pltpu.make_async_copy(w_ref.at[:, cols], w.at[s], w_s.at[s])

    def load_x(j):
        cols = pl.ds(pl.multiple_of(j * share, HD), share)
        return pltpu.make_async_copy(wx_ref.at[:, cols], wx.at[j], w_s.at[4 + j])

    def rows_of(r):
        return pl.ds(pl.multiple_of(r * step, step), step)

    def send(kind, src, dst, r, dev):
        return pltpu.make_async_remote_copy(src_ref=src, dst_ref=dst.at[r], send_sem=send_s.at[kind, r],
                                            recv_sem=rec_s.at[kind, r], device_id={"tensor": dev},
                                            device_id_type=MESH)

    def c_att(r):
        return send(0, a_ref.at[rows_of(r), :], am, r, mate)

    def c_part(r):
        return send(1, ps.at[r], pm, r, mate)

    def c_fo(r):
        return send(2, tfo.at[r], sfo, r, peer)

    def c_pe(r):
        return send(3, tpe.at[r], spe, r, peer)

    def c_fin(r):
        return send(4, fs.at[r], f, r, mate)

    def dot(lhs, rhs):
        return jnp.dot(lhs, rhs, preferred_element_type=jnp.float32)

    def mine(r):
        return a_ref[rows_of(r), :]

    def each(fn):
        def one(r, _):
            fn(r)
            return 0

        lax.fori_loop(0, chunks, one, 0)

    def store(r, total):
        o_ref[rows_of(r), :] = (
            res_ref[rows_of(r), :].astype(jnp.float32) + gate_ref[...] * total
        ).astype(o_ref.dtype)

    barrier = pltpu.get_barrier_semaphore()
    pl.semaphore_signal(barrier, inc=1, device_id={"tensor": mate}, device_id_type=MESH)

    @pl.when(inner)
    def _():
        pl.semaphore_signal(barrier, inc=1, device_id={"tensor": peer}, device_id_type=MESH)
        pl.semaphore_wait(barrier, 2)
        order = (load(far + jfo), load_x(jfo), load(far + jpe), load_x(jpe), load(mate), load(z))
        for copy in order:
            copy.start()
        for copy in order[:2]:
            copy.wait()

        @each
        def _(r):
            c_att(r).wait_recv()
            tfo[r] = (dot(mine(r), w[far + jfo]) + dot(am[r], wx[jfo])).astype(jnp.bfloat16)
            c_fo(r).start()

        for copy in order[2:]:
            copy.wait()

        @each
        def _(r):
            tpe[r] = (dot(mine(r), w[far + jpe]) + dot(am[r], wx[jpe])).astype(jnp.bfloat16)
            c_pe(r).start()
            own_s[r] = dot(mine(r), w[mate])
            c_fo(r).wait_recv()
            fs[r] = (own_s[r] + sfo[r].astype(jnp.float32)).astype(jnp.bfloat16)
            c_fin(r).start()

        @each
        def _(r):
            own_s[r] = dot(mine(r), w[z])

        @each
        def _(r):
            c_part(r).wait_recv()
            c_pe(r).wait_recv()
            store(r, own_s[r] + pm[r].astype(jnp.float32) + spe[r].astype(jnp.float32))

        @each
        def _(r):
            c_fo(r).wait_send()
            c_pe(r).wait_send()
            c_fin(r).wait_send()

    @pl.when(outer)
    def _():
        pl.semaphore_wait(barrier, 1)

        @each
        def _(r):
            c_att(r).start()

        order = (load(mate), load(z))
        for copy in order:
            copy.start()
        for copy in order:
            copy.wait()

        @each
        def _(r):
            ps[r] = dot(mine(r), w[mate]).astype(jnp.bfloat16)
            c_part(r).start()
            own_s[r] = dot(mine(r), w[z])

        @each
        def _(r):
            c_fin(r).wait_recv()
            store(r, own_s[r] + f[r].astype(jnp.float32))

        @each
        def _(r):
            c_att(r).wait_send()
            c_part(r).wait_send()


def line_project(attended, weight_mate, out_weight, residual, gate):
    rows, cols = attended.shape
    share = out_weight.shape[1] // 4
    chunks = rows // 128
    vmem = pl.BlockSpec(memory_space=pltpu.VMEM)
    hbm = pl.BlockSpec(memory_space=pl.ANY)
    dma = pltpu.SemaphoreType.DMA
    bf16, f32 = jnp.bfloat16, jnp.float32
    blocks = [pltpu.VMEM((chunks, 128, share), bf16) for _ in range(7)]
    return pl.pallas_call(
        project_kernel,
        in_specs=[vmem, hbm, hbm, vmem, vmem],
        out_specs=vmem,
        out_shape=jax.ShapeDtypeStruct((rows, share), bf16),
        scratch_shapes=[
            pltpu.VMEM((4, cols, share), bf16),
            pltpu.VMEM((2, cols, share), bf16),
            pltpu.VMEM((chunks, 128, cols), bf16),
            *blocks,
            pltpu.VMEM((chunks, 128, share), bf16),
            pltpu.VMEM((chunks, 128, share), f32),
            dma((6,)),
            dma((5, chunks)),
            dma((5, chunks)),
        ],
        compiler_params=pltpu.CompilerParams(
            collective_id=2, has_side_effects=True, vmem_limit_bytes=56 * 2**20
        ),
        name="line_project",
    )(attended, out_weight, weight_mate, residual, gate[None, :])


def general_body(n, query, key_fresh, value_fresh, key_stale, value_stale, out_weight, residual, gate):
    rows, cols = query.shape
    if n == 8 and lax.axis_size("tensor") == 4 and cols % (2 * HD) == 0:
        attended, weight_mate = paired_attention(
            query, key_fresh, value_fresh, key_stale, value_stale, out_weight
        )
        return line_project(attended, weight_mate, out_weight, residual, gate)
    keys = lax.all_gather(key_stale, "patch", axis=0, tiled=True)
    values = lax.all_gather(value_stale, "patch", axis=0, tiled=True)
    local = pl.BlockSpec((rows, HD), lambda h: (0, h))
    whole = pl.BlockSpec((rows * n, HD), lambda h: (0, h))
    attended = pl.pallas_call(
        functools.partial(flash_kernel, n),
        grid=(cols // HD,),
        in_specs=[local, local, local, whole, whole],
        out_specs=local,
        out_shape=jax.ShapeDtypeStruct((rows, cols), jnp.bfloat16),
        compiler_params=pltpu.CompilerParams(vmem_limit_bytes=48 * 2**20),
        name="flash",
    )(query, key_fresh, value_fresh, keys, values)
    return project(attended, out_weight, residual, gate)


def project(attended, out_weight, residual, gate):
    partial = jnp.dot(attended, out_weight, preferred_element_type=jnp.float32).astype(jnp.bfloat16)
    mine = lax.psum_scatter(partial, "tensor", scatter_dimension=1, tiled=True).astype(jnp.float32)
    return (residual.astype(jnp.float32) + gate[None, :] * mine).astype(jnp.bfloat16)


def solution(mesh):
    n = mesh.shape["patch"]
    both = P("patch", "tensor")
    return jax.shard_map(
        functools.partial(general_body, n),
        mesh=mesh,
        in_specs=(both,) * 5 + (P("tensor", None), both, P("tensor")),
        out_specs=both,
        check_vma=False,
    )
```

```python
import functools
import math

import jax
import jax.numpy as jnp
from jax import lax
from jax.experimental import pallas as pl
from jax.experimental.pallas import tpu as pltpu
from jax.sharding import PartitionSpec as P

HD = 128
SCALE = HD ** -0.5 * math.log2(math.e)


def attend_block(q, k, v, m_old, acc_old):
    s = lax.dot_general(q, k, (((1,), (1,)), ((), ())), preferred_element_type=jnp.float32) * SCALE
    m_new = jnp.maximum(m_old, jnp.max(s, axis=-1, keepdims=True))
    p = jnp.exp2(s - jnp.tile(m_new, (1, s.shape[1] // HD))).astype(jnp.bfloat16)
    v1 = jnp.concatenate([v, jnp.ones_like(v)], axis=1)
    add = jnp.dot(p, v1, preferred_element_type=jnp.float32)
    return m_new, acc_old * jnp.tile(jnp.exp2(m_old - m_new), (1, 2)) + add


def flash_kernel(n, q_ref, kf_ref, vf_ref, ks_ref, vs_ref, o_ref):
    rows = q_ref.shape[0]
    own = lax.axis_index("patch")
    q = q_ref[...]
    m0 = jnp.full((rows, HD), -1e30, jnp.float32)
    a0 = jnp.zeros((rows, 2 * HD), jnp.float32)
    state = attend_block(q, kf_ref[...], vf_ref[...], m0, a0)

    def inner(j, state):
        first = pl.multiple_of(lax.rem(own + j, n) * rows, rows)
        return attend_block(q, ks_ref[pl.ds(first, rows), :], vs_ref[pl.ds(first, rows), :], *state)

    m, acc = lax.fori_loop(1, n, inner, state)
    o_ref[...] = (acc[:, :HD] / acc[:, HD:]).astype(o_ref.dtype)


MESH = pl.DeviceIdType.MESH
FRESH, PX, PC, PXC, OWN, PY, PYX, PYC, PYXC = range(9)


def attend_kernel(q_ref, kf_ref, vf_ref, ks_ref, vs_ref, w_ref, o_ref, wx_ref, kv, qx, osend, orecv, lsend, lrecv,
                  m_s, acc_s, first_s, first_q, fwd_s, ret_s, rec_kv, rec_q, rec_o, w_s, rec_w):
    own = lax.axis_index("patch")
    c, x, y = lax.rem(own, 2), lax.rem(own // 2, 2), own // 4

    def at(ky, kx, kc):
        return lax.rem(y + ky, 2) * 4 + lax.rem(x + kx, 2) * 2 + lax.rem(c + kc, 2)

    pc, px, py = at(0, 0, 1), at(0, 1, 0), at(1, 0, 0)
    half = kv.shape[0]
    rows = q_ref.shape[0]
    tile = rows // 2
    z = lax.axis_index("tensor")
    mate = z + 1 - 2 * lax.rem(z, 2)
    outer = lax.rem(z, 3) == 0
    width = wx_ref.shape[1]

    def head_cols(hx, i):
        return pl.ds(pl.multiple_of((hx * half + i) * HD, HD), HD)

    def send(src, dst, ssem, rsem, dev):
        return pltpu.make_async_remote_copy(src_ref=src, dst_ref=dst, send_sem=ssem, recv_sem=rsem,
                                            device_id={"patch": dev}, device_id_type=MESH)

    def firsts(i):
        mine, theirs = head_cols(x, i), head_cols(1 - x, i)
        out = [send(q_ref.at[:, theirs], qx.at[i], first_q.at[i], rec_q.at[i], px)]
        for t, src in enumerate((ks_ref, vs_ref)):
            out.append(send(src.at[:, theirs], kv.at[i, t, PX], first_s.at[0, i, t], rec_kv.at[i, PX], px))
            out.append(send(src.at[:, mine], kv.at[i, t, PY], first_s.at[1, i, t], rec_kv.at[i, PY], py))
            out.append(send(src.at[:, mine], kv.at[i, t, PC], first_s.at[2, i, t], rec_kv.at[i, PC], pc))
        return out

    def locals_of(i):
        mine = head_cols(x, i)
        out = []
        for t, (new, old) in enumerate(((kf_ref, ks_ref), (vf_ref, vs_ref))):
            out.append(pltpu.make_async_copy(new.at[:, mine], kv.at[i, t, FRESH], first_s.at[3, i, t]))
            out.append(pltpu.make_async_copy(old.at[:, mine], kv.at[i, t, OWN], first_s.at[4, i, t]))
        return out

    def weight_rows(core, i):
        return pl.ds(pl.multiple_of((core * half + i) * HD, HD), HD)

    def weight_out(i):
        cols = pl.ds(pl.multiple_of((1 - z // 2) * width, HD), width)
        return pltpu.make_async_remote_copy(
            src_ref=w_ref.at[weight_rows(c, i), cols], dst_ref=wx_ref.at[weight_rows(c, i), :],
            send_sem=w_s.at[i], recv_sem=rec_w.at[0, i], device_id={"tensor": mate}, device_id_type=MESH)

    def weight_on(i, core):
        part = wx_ref.at[weight_rows(core, i), :]
        return send(part, part, w_s.at[i], rec_w.at[1, i], pc)

    def weight_pass(i):
        @pl.when(jnp.logical_not(outer))
        def _():
            weight_out(i).wait_recv()
            weight_on(i, c).start()

    def start_first(i):
        for copy in firsts(i) + locals_of(i):
            copy.start()

        @pl.when(outer)
        def _():
            weight_out(i).start()

    def fwd(kind, i):
        slot, to, dev = ((PX, PYX, py), (PX, PXC, pc), (PY, PYC, pc), (PYX, PYXC, pc))[kind]
        return send(kv.at[i, :, slot], kv.at[i, :, to], fwd_s.at[kind, i], rec_kv.at[i, to], dev)

    def arrived(i, slot):
        part = kv.at[i, :, slot]
        send(part, part, fwd_s.at[0, i], rec_kv.at[i, slot], pc).wait_recv()

    def back(i):
        return (send(osend.at[i], orecv.at[i], ret_s.at[0, i], rec_o.at[0, i], px),
                send(lsend.at[i], lrecv.at[i], ret_s.at[1, i], rec_o.at[1, i], px))

    def pass_on_x(i):
        arrived(i, PX)
        fwd(0, i).start()
        fwd(1, i).start()

    def query_tile(i, t):
        if t < 2:
            return q_ref[pl.ds(t * tile, tile), head_cols(x, i)]
        return qx[i, pl.ds((t - 2) * tile, tile), :]

    def keys_values(i, first, count):
        return [kv[i, t, pl.ds(first, count)].reshape(count * rows, HD) for t in range(2)]

    def start_state():
        return jnp.full((tile, HD), -1e30, jnp.float32), jnp.zeros((tile, 2 * HD), jnp.float32)

    def near(i, t, first, count):
        m_s[t], acc_s[t] = attend_block(query_tile(i, t), *keys_values(i, first, count), *start_state())

    def merge(i):
        theirs = head_cols(1 - x, i)
        for copy in back(i):
            copy.wait_recv()
        for t in range(2):
            part = pl.ds(t * tile, tile)
            m = jnp.broadcast_to(lrecv[i, 0:1, part], (HD, tile)).T
            acc = jnp.concatenate([orecv[i, part, :].astype(jnp.float32), jnp.ones((tile, HD), jnp.float32)], axis=1)
            m, acc = attend_block(q_ref[part, theirs], kf_ref[:, theirs], vf_ref[:, theirs], m, acc)
            o_ref[part, theirs] = (acc[:, :HD] / acc[:, HD:]).astype(o_ref.dtype)

    barrier = pltpu.get_barrier_semaphore()
    for dev in (pc, px, py):
        pl.semaphore_signal(barrier, inc=1, device_id={"patch": dev}, device_id_type=MESH)
    pl.semaphore_signal(barrier, inc=1, device_id={"tensor": mate}, device_id_type=MESH)
    pl.semaphore_wait(barrier, 4)

    start_first(0)
    start_first(1)

    def one_head(i, _):
        @pl.when(i + 2 < half)
        def _():
            start_first(i + 2)

        mine = head_cols(x, i)

        @pl.when(i == 0)
        def _():
            pass_on_x(0)

        for copy in locals_of(i):
            copy.wait()
        arrived(i, PC)
        arrived(i, PXC)
        for t in range(2):
            near(i, t, FRESH, 4)

        @pl.when(i + 1 < half)
        def _():
            pass_on_x(i + 1)

        arrived(i, PY)
        fwd(2, i).start()
        arrived(i, PYX)
        fwd(3, i).start()
        firsts(i)[0].wait_recv()
        for t in range(2, 4):
            near(i, t, PC, 3)

        @pl.when(i > 0)
        def _():
            merge(i - 1)

        arrived(i, PYC)
        arrived(i, PYXC)
        for t in range(4):
            m, acc = attend_block(query_tile(i, t), *keys_values(i, PY, 4), m_s[t], acc_s[t])
            total = acc[:, HD:]
            out = (acc[:, :HD] / total).astype(o_ref.dtype)
            if t < 2:
                o_ref[pl.ds(t * tile, tile), mine] = out
            else:
                part = pl.ds((t - 2) * tile, tile)
                osend[i, part, :] = out
                lsend[i, :, part] = (m + jnp.log2(total)).T[0:8, :]
        for copy in back(i):
            copy.start()

        @pl.when(i > 0)
        def _():
            weight_pass(i - 1)

        return 0

    lax.fori_loop(0, half, one_head, 0)
    merge(half - 1)
    weight_pass(half - 1)

    def finish(i, _):
        @pl.when(outer)
        def _():
            weight_out(i).wait_send()

        @pl.when(jnp.logical_not(outer))
        def _():
            weight_on(i, c).wait_send()
            weight_on(i, 1 - c).wait_recv()

        firsts_i = firsts(i)
        firsts_i[0].wait_send()
        for t in range(2):
            for k in range(3):
                firsts_i[1 + 3 * t + k].wait_send()
        for kind in range(4):
            fwd(kind, i).wait_send()
        for copy in back(i):
            copy.wait_send()
        return 0

    lax.fori_loop(0, half, finish, 0)


def paired_attention(query, key_fresh, value_fresh, key_stale, value_stale, out_weight):
    rows, cols = query.shape
    half = cols // HD // 2
    vmem = pl.BlockSpec(memory_space=pltpu.VMEM)
    hbm = pl.BlockSpec(memory_space=pl.ANY)
    dma = pltpu.SemaphoreType.DMA
    bf16, f32 = jnp.bfloat16, jnp.float32
    return pl.pallas_call(
        attend_kernel,
        in_specs=[vmem, vmem, vmem, hbm, hbm, hbm],
        out_specs=[vmem, hbm],
        out_shape=[jax.ShapeDtypeStruct((rows, cols), bf16),
                   jax.ShapeDtypeStruct((cols, out_weight.shape[1] // 2), bf16)],
        scratch_shapes=[
            pltpu.VMEM((half, 2, 9, rows, HD), bf16),
            pltpu.VMEM((half, rows, HD), bf16),
            pltpu.VMEM((half, rows, HD), bf16),
            pltpu.VMEM((half, rows, HD), bf16),
            pltpu.VMEM((half, 8, rows), f32),
            pltpu.VMEM((half, 8, rows), f32),
            pltpu.VMEM((4, rows // 2, HD), f32),
            pltpu.VMEM((4, rows // 2, 2 * HD), f32),
            dma((5, half, 2)),
            dma((half,)),
            dma((4, half)),
            dma((2, half)),
            dma((half, 9)),
            dma((half,)),
            dma((2, half)),
            dma((half,)),
            dma((2, half)),
        ],
        compiler_params=pltpu.CompilerParams(
            collective_id=1, has_side_effects=True, vmem_limit_bytes=56 * 2**20
        ),
        name="paired_attention",
    )(query, key_fresh, value_fresh, key_stale, value_stale, out_weight)


def project_kernel(a_ref, w_ref, wx_ref, res_ref, gate_ref, o_ref, w, wx, am, pm, sfo, spe, f, tfo, tpe,
                   fs, ps, own_s, w_s, send_s, rec_s):
    z = lax.axis_index("tensor")
    mate = z + 1 - 2 * lax.rem(z, 2)
    outer = lax.rem(z, 3) == 0
    inner = jnp.logical_not(outer)
    peer = 3 - z
    far = 2 * (1 - z // 2)
    jfo, jpe = lax.rem(z, 2), 1 - lax.rem(z, 2)
    chunks, step, share = am.shape

    def load(s):
        cols = pl.ds(pl.multiple_of(s * share, HD), share)
        return pltpu.make_async_copy(w_ref.at[:, cols], w.at[s], w_s.at[s])

    def load_x(j):
        cols = pl.ds(pl.multiple_of(j * share, HD), share)
        return pltpu.make_async_copy(wx_ref.at[:, cols], wx.at[j], w_s.at[4 + j])

    def rows_of(r):
        return pl.ds(pl.multiple_of(r * step, step), step)

    def send(kind, src, dst, r, dev):
        return pltpu.make_async_remote_copy(src_ref=src, dst_ref=dst.at[r], send_sem=send_s.at[kind, r],
                                            recv_sem=rec_s.at[kind, r], device_id={"tensor": dev},
                                            device_id_type=MESH)

    def c_att(r):
        return send(0, a_ref.at[rows_of(r), :], am, r, mate)

    def c_part(r):
        return send(1, ps.at[r], pm, r, mate)

    def c_fo(r):
        return send(2, tfo.at[r], sfo, r, peer)

    def c_pe(r):
        return send(3, tpe.at[r], spe, r, peer)

    def c_fin(r):
        return send(4, fs.at[r], f, r, mate)

    def dot(lhs, rhs):
        return jnp.dot(lhs, rhs, preferred_element_type=jnp.float32)

    def mine(r):
        return a_ref[rows_of(r), :]

    def each(fn):
        def one(r, _):
            fn(r)
            return 0

        lax.fori_loop(0, chunks, one, 0)

    def store(r, total):
        o_ref[rows_of(r), :] = (
            res_ref[rows_of(r), :].astype(jnp.float32) + gate_ref[...][None, :] * total
        ).astype(o_ref.dtype)

    barrier = pltpu.get_barrier_semaphore()
    pl.semaphore_signal(barrier, inc=1, device_id={"tensor": mate}, device_id_type=MESH)

    @pl.when(inner)
    def _():
        pl.semaphore_signal(barrier, inc=1, device_id={"tensor": peer}, device_id_type=MESH)
        pl.semaphore_wait(barrier, 2)
        order = (load(far + jfo), load_x(jfo), load(far + jpe), load_x(jpe), load(mate), load(z))
        for copy in order:
            copy.start()
        for copy in order[:2]:
            copy.wait()

        @each
        def _(r):
            c_att(r).wait_recv()
            tfo[r] = (dot(mine(r), w[far + jfo]) + dot(am[r], wx[jfo])).astype(jnp.bfloat16)
            c_fo(r).start()

        for copy in order[2:]:
            copy.wait()

        @each
        def _(r):
            tpe[r] = (dot(mine(r), w[far + jpe]) + dot(am[r], wx[jpe])).astype(jnp.bfloat16)
            c_pe(r).start()
            own_s[r] = dot(mine(r), w[mate])
            c_fo(r).wait_recv()
            fs[r] = (own_s[r] + sfo[r].astype(jnp.float32)).astype(jnp.bfloat16)
            c_fin(r).start()

        @each
        def _(r):
            own_s[r] = dot(mine(r), w[z])

        @each
        def _(r):
            c_part(r).wait_recv()
            c_pe(r).wait_recv()
            store(r, own_s[r] + pm[r].astype(jnp.float32) + spe[r].astype(jnp.float32))

        @each
        def _(r):
            c_fo(r).wait_send()
            c_pe(r).wait_send()
            c_fin(r).wait_send()

    @pl.when(outer)
    def _():
        pl.semaphore_wait(barrier, 1)

        @each
        def _(r):
            c_att(r).start()

        order = (load(mate), load(z))
        for copy in order:
            copy.start()
        for copy in order:
            copy.wait()

        @each
        def _(r):
            ps[r] = dot(mine(r), w[mate]).astype(jnp.bfloat16)
            c_part(r).start()
            own_s[r] = dot(mine(r), w[z])

        @each
        def _(r):
            c_fin(r).wait_recv()
            store(r, own_s[r] + f[r].astype(jnp.float32))

        @each
        def _(r):
            c_att(r).wait_send()
            c_part(r).wait_send()


def line_project(attended, weight_mate, out_weight, residual, gate):
    rows, cols = attended.shape
    share = out_weight.shape[1] // 4
    chunks = rows // 128
    vmem = pl.BlockSpec(memory_space=pltpu.VMEM)
    hbm = pl.BlockSpec(memory_space=pl.ANY)
    dma = pltpu.SemaphoreType.DMA
    bf16, f32 = jnp.bfloat16, jnp.float32
    blocks = [pltpu.VMEM((chunks, 128, share), bf16) for _ in range(7)]
    return pl.pallas_call(
        project_kernel,
        in_specs=[vmem, hbm, hbm, vmem, vmem],
        out_specs=vmem,
        out_shape=jax.ShapeDtypeStruct((rows, share), bf16),
        scratch_shapes=[
            pltpu.VMEM((4, cols, share), bf16),
            pltpu.VMEM((2, cols, share), bf16),
            pltpu.VMEM((chunks, 128, cols), bf16),
            *blocks,
            pltpu.VMEM((chunks, 128, share), bf16),
            pltpu.VMEM((chunks, 128, share), f32),
            dma((6,)),
            dma((5, chunks)),
            dma((5, chunks)),
        ],
        compiler_params=pltpu.CompilerParams(
            collective_id=2, has_side_effects=True, vmem_limit_bytes=56 * 2**20
        ),
        name="line_project",
    )(attended, out_weight, weight_mate, residual, gate)


def general_body(n, query, key_fresh, value_fresh, key_stale, value_stale, out_weight, residual, gate):
    rows, cols = query.shape
    if n == 8 and lax.axis_size("tensor") == 4 and cols % (2 * HD) == 0:
        attended, weight_mate = paired_attention(
            query, key_fresh, value_fresh, key_stale, value_stale, out_weight
        )
        return line_project(attended, weight_mate, out_weight, residual, gate)
    keys = lax.all_gather(key_stale, "patch", axis=0, tiled=True)
    values = lax.all_gather(value_stale, "patch", axis=0, tiled=True)
    local = pl.BlockSpec((rows, HD), lambda h: (0, h))
    whole = pl.BlockSpec((rows * n, HD), lambda h: (0, h))
    attended = pl.pallas_call(
        functools.partial(flash_kernel, n),
        grid=(cols // HD,),
        in_specs=[local, local, local, whole, whole],
        out_specs=local,
        out_shape=jax.ShapeDtypeStruct((rows, cols), jnp.bfloat16),
        compiler_params=pltpu.CompilerParams(vmem_limit_bytes=48 * 2**20),
        name="flash",
    )(query, key_fresh, value_fresh, keys, values)
    return project(attended, out_weight, residual, gate)


def project(attended, out_weight, residual, gate):
    partial = jnp.dot(attended, out_weight, preferred_element_type=jnp.float32).astype(jnp.bfloat16)
    mine = lax.psum_scatter(partial, "tensor", scatter_dimension=1, tiled=True).astype(jnp.float32)
    return (residual.astype(jnp.float32) + gate[None, :] * mine).astype(jnp.bfloat16)


def solution(mesh):
    n = mesh.shape["patch"]
    both = P("patch", "tensor")
    return jax.shard_map(
        functools.partial(general_body, n),
        mesh=mesh,
        in_specs=(both,) * 5 + (P("tensor", None), both, P("tensor")),
        out_specs=both,
        check_vma=False,
    )
```

```python
import functools
import math

import jax
import jax.numpy as jnp
from jax import lax
from jax.experimental import pallas as pl
from jax.experimental.pallas import tpu as pltpu
from jax.sharding import PartitionSpec as P

HD = 128
SCALE = HD ** -0.5 * math.log2(math.e)


def attend_block(q, k, v, m_old, acc_old):
    s = lax.dot_general(q, k, (((1,), (1,)), ((), ())), preferred_element_type=jnp.float32) * SCALE
    m_new = jnp.maximum(m_old, jnp.max(s, axis=-1, keepdims=True))
    p = jnp.exp2(s - jnp.tile(m_new, (1, s.shape[1] // HD))).astype(jnp.bfloat16)
    v1 = jnp.concatenate([v, jnp.ones_like(v)], axis=1)
    add = jnp.dot(p, v1, preferred_element_type=jnp.float32)
    return m_new, acc_old * jnp.tile(jnp.exp2(m_old - m_new), (1, 2)) + add


def flash_kernel(n, q_ref, kf_ref, vf_ref, ks_ref, vs_ref, o_ref):
    rows = q_ref.shape[0]
    own = lax.axis_index("patch")
    q = q_ref[...]
    m0 = jnp.full((rows, HD), -1e30, jnp.float32)
    a0 = jnp.zeros((rows, 2 * HD), jnp.float32)
    state = attend_block(q, kf_ref[...], vf_ref[...], m0, a0)

    def inner(j, state):
        first = pl.multiple_of(lax.rem(own + j, n) * rows, rows)
        return attend_block(q, ks_ref[pl.ds(first, rows), :], vs_ref[pl.ds(first, rows), :], *state)

    m, acc = lax.fori_loop(1, n, inner, state)
    o_ref[...] = (acc[:, :HD] / acc[:, HD:]).astype(o_ref.dtype)


MESH = pl.DeviceIdType.MESH
FRESH, PX, PC, PXC, OWN, PY, PYX, PYC, PYXC = range(9)


def attend_kernel(q_ref, kf_ref, vf_ref, ks_ref, vs_ref, w_ref, o_ref, wx_ref, kv, qx, osend, orecv, lsend, lrecv,
                  m_s, acc_s, first_s, first_q, fwd_s, ret_s, rec_kv, rec_q, rec_o, w_s, rec_w):
    own = lax.axis_index("patch")
    c, x, y = lax.rem(own, 2), lax.rem(own // 2, 2), own // 4

    def at(ky, kx, kc):
        return lax.rem(y + ky, 2) * 4 + lax.rem(x + kx, 2) * 2 + lax.rem(c + kc, 2)

    pc, px, py = at(0, 0, 1), at(0, 1, 0), at(1, 0, 0)
    half = kv.shape[0]
    rows = q_ref.shape[0]
    tile = rows // 2
    z = lax.axis_index("tensor")
    mate = z + 1 - 2 * lax.rem(z, 2)
    outer = lax.rem(z, 3) == 0
    width = wx_ref.shape[1]

    def head_cols(hx, i):
        return pl.ds(pl.multiple_of((hx * half + i) * HD, HD), HD)

    def send(src, dst, ssem, rsem, dev):
        return pltpu.make_async_remote_copy(src_ref=src, dst_ref=dst, send_sem=ssem, recv_sem=rsem,
                                            device_id={"patch": dev}, device_id_type=MESH)

    def firsts(i):
        mine, theirs = head_cols(x, i), head_cols(1 - x, i)
        out = [send(q_ref.at[:, theirs], qx.at[i], first_q.at[i], rec_q.at[i], px)]
        for t, src in enumerate((ks_ref, vs_ref)):
            out.append(send(src.at[:, theirs], kv.at[i, t, PX], first_s.at[0, i, t], rec_kv.at[i, PX], px))
            out.append(send(src.at[:, mine], kv.at[i, t, PY], first_s.at[1, i, t], rec_kv.at[i, PY], py))
            out.append(send(src.at[:, mine], kv.at[i, t, PC], first_s.at[2, i, t], rec_kv.at[i, PC], pc))
        return out

    def locals_of(i):
        mine = head_cols(x, i)
        out = []
        for t, (new, old) in enumerate(((kf_ref, ks_ref), (vf_ref, vs_ref))):
            out.append(pltpu.make_async_copy(new.at[:, mine], kv.at[i, t, FRESH], first_s.at[3, i, t]))
            out.append(pltpu.make_async_copy(old.at[:, mine], kv.at[i, t, OWN], first_s.at[4, i, t]))
        return out

    def weight_rows(core, i):
        return pl.ds(pl.multiple_of((core * half + i) * HD, HD), HD)

    def weight_out(i):
        cols = pl.ds(pl.multiple_of((1 - z // 2) * width, HD), width)
        return pltpu.make_async_remote_copy(
            src_ref=w_ref.at[weight_rows(c, i), cols], dst_ref=wx_ref.at[weight_rows(c, i), :],
            send_sem=w_s.at[i], recv_sem=rec_w.at[0, i], device_id={"tensor": mate}, device_id_type=MESH)

    def weight_on(i, core):
        part = wx_ref.at[weight_rows(core, i), :]
        return send(part, part, w_s.at[i], rec_w.at[1, i], pc)

    def weight_pass(i):
        @pl.when(jnp.logical_not(outer))
        def _():
            weight_out(i).wait_recv()
            weight_on(i, c).start()

    def start_first(i):
        for copy in firsts(i) + locals_of(i):
            copy.start()

    def start_weight(i):
        @pl.when(outer)
        def _():
            weight_out(i).start()

    def fwd(kind, i):
        slot, to, dev = ((PX, PYX, py), (PX, PXC, pc), (PY, PYC, pc), (PYX, PYXC, pc))[kind]
        return send(kv.at[i, :, slot], kv.at[i, :, to], fwd_s.at[kind, i], rec_kv.at[i, to], dev)

    def arrived(i, slot):
        part = kv.at[i, :, slot]
        send(part, part, fwd_s.at[0, i], rec_kv.at[i, slot], pc).wait_recv()

    def back(i):
        return (send(osend.at[i], orecv.at[i], ret_s.at[0, i], rec_o.at[0, i], px),
                send(lsend.at[i], lrecv.at[i], ret_s.at[1, i], rec_o.at[1, i], px))

    def pass_on_x(i):
        arrived(i, PX)
        fwd(0, i).start()
        fwd(1, i).start()

    def query_tile(i, t):
        if t < 2:
            return q_ref[pl.ds(t * tile, tile), head_cols(x, i)]
        return qx[i, pl.ds((t - 2) * tile, tile), :]

    def keys_values(i, first, count):
        return [kv[i, t, pl.ds(first, count)].reshape(count * rows, HD) for t in range(2)]

    def start_state():
        return jnp.full((tile, HD), -1e30, jnp.float32), jnp.zeros((tile, 2 * HD), jnp.float32)

    def near(i, t, first, count):
        m_s[t], acc_s[t] = attend_block(query_tile(i, t), *keys_values(i, first, count), *start_state())

    def merge(i):
        theirs = head_cols(1 - x, i)
        for copy in back(i):
            copy.wait_recv()
        for t in range(2):
            part = pl.ds(t * tile, tile)
            m = jnp.broadcast_to(lrecv[i, 0:1, part], (HD, tile)).T
            acc = jnp.concatenate([orecv[i, part, :].astype(jnp.float32), jnp.ones((tile, HD), jnp.float32)], axis=1)
            m, acc = attend_block(q_ref[part, theirs], kf_ref[:, theirs], vf_ref[:, theirs], m, acc)
            o_ref[part, theirs] = (acc[:, :HD] / acc[:, HD:]).astype(o_ref.dtype)

    barrier = pltpu.get_barrier_semaphore()
    for dev in (pc, px, py):
        pl.semaphore_signal(barrier, inc=1, device_id={"patch": dev}, device_id_type=MESH)
    pl.semaphore_signal(barrier, inc=1, device_id={"tensor": mate}, device_id_type=MESH)
    pl.semaphore_wait(barrier, 4)

    start_first(0)
    start_weight(0)

    def one_head(i, _):
        @pl.when(i + 1 < half)
        def _():
            start_weight(i + 1)

        mine = head_cols(x, i)

        @pl.when(i == 0)
        def _():
            pass_on_x(0)
            if half > 1:
                start_first(1)

        for copy in locals_of(i):
            copy.wait()
        arrived(i, PC)
        arrived(i, PXC)
        for t in range(2):
            near(i, t, FRESH, 4)

        @pl.when(i + 1 < half)
        def _():
            pass_on_x(i + 1)

        @pl.when(i + 2 < half)
        def _():
            start_first(i + 2)

        arrived(i, PY)
        fwd(2, i).start()
        arrived(i, PYX)
        fwd(3, i).start()
        firsts(i)[0].wait_recv()
        for t in range(2, 4):
            near(i, t, PC, 3)

        @pl.when(i > 0)
        def _():
            merge(i - 1)

        arrived(i, PYC)
        arrived(i, PYXC)
        for t in range(4):
            m, acc = attend_block(query_tile(i, t), *keys_values(i, PY, 4), m_s[t], acc_s[t])
            total = acc[:, HD:]
            out = (acc[:, :HD] / total).astype(o_ref.dtype)
            if t < 2:
                o_ref[pl.ds(t * tile, tile), mine] = out
            else:
                part = pl.ds((t - 2) * tile, tile)
                osend[i, part, :] = out
                lsend[i, :, part] = (m + jnp.log2(total)).T[0:8, :]
        for copy in back(i):
            copy.start()

        @pl.when(i > 1)
        def _():
            weight_pass(i - 2)

        return 0

    lax.fori_loop(0, half, one_head, 0)
    for i in range(max(half - 2, 0), half - 1):
        weight_pass(i)
    merge(half - 1)
    weight_pass(half - 1)

    def finish(i, _):
        @pl.when(outer)
        def _():
            weight_out(i).wait_send()

        @pl.when(jnp.logical_not(outer))
        def _():
            weight_on(i, c).wait_send()
            weight_on(i, 1 - c).wait_recv()

        firsts_i = firsts(i)
        firsts_i[0].wait_send()
        for t in range(2):
            for k in range(3):
                firsts_i[1 + 3 * t + k].wait_send()
        for kind in range(4):
            fwd(kind, i).wait_send()
        for copy in back(i):
            copy.wait_send()
        return 0

    lax.fori_loop(0, half, finish, 0)


def paired_attention(query, key_fresh, value_fresh, key_stale, value_stale, out_weight):
    rows, cols = query.shape
    half = cols // HD // 2
    vmem = pl.BlockSpec(memory_space=pltpu.VMEM)
    hbm = pl.BlockSpec(memory_space=pl.ANY)
    dma = pltpu.SemaphoreType.DMA
    bf16, f32 = jnp.bfloat16, jnp.float32
    return pl.pallas_call(
        attend_kernel,
        in_specs=[vmem, vmem, vmem, hbm, hbm, hbm],
        out_specs=[vmem, hbm],
        out_shape=[jax.ShapeDtypeStruct((rows, cols), bf16),
                   jax.ShapeDtypeStruct((cols, out_weight.shape[1] // 2), bf16)],
        scratch_shapes=[
            pltpu.VMEM((half, 2, 9, rows, HD), bf16),
            pltpu.VMEM((half, rows, HD), bf16),
            pltpu.VMEM((half, rows, HD), bf16),
            pltpu.VMEM((half, rows, HD), bf16),
            pltpu.VMEM((half, 8, rows), f32),
            pltpu.VMEM((half, 8, rows), f32),
            pltpu.VMEM((4, rows // 2, HD), f32),
            pltpu.VMEM((4, rows // 2, 2 * HD), f32),
            dma((5, half, 2)),
            dma((half,)),
            dma((4, half)),
            dma((2, half)),
            dma((half, 9)),
            dma((half,)),
            dma((2, half)),
            dma((half,)),
            dma((2, half)),
        ],
        compiler_params=pltpu.CompilerParams(
            collective_id=1, has_side_effects=True, vmem_limit_bytes=56 * 2**20
        ),
        name="paired_attention",
    )(query, key_fresh, value_fresh, key_stale, value_stale, out_weight)


def project_kernel(a_ref, w_ref, wx_ref, res_ref, gate_ref, o_ref, w, wx, am, pm, sfo, spe, f, tfo, tpe,
                   fs, ps, own_s, w_s, send_s, rec_s):
    z = lax.axis_index("tensor")
    mate = z + 1 - 2 * lax.rem(z, 2)
    outer = lax.rem(z, 3) == 0
    inner = jnp.logical_not(outer)
    peer = 3 - z
    far = 2 * (1 - z // 2)
    jfo, jpe = lax.rem(z, 2), 1 - lax.rem(z, 2)
    chunks, step, share = am.shape

    def load(s):
        cols = pl.ds(pl.multiple_of(s * share, HD), share)
        return pltpu.make_async_copy(w_ref.at[:, cols], w.at[s], w_s.at[s])

    def load_x(j):
        cols = pl.ds(pl.multiple_of(j * share, HD), share)
        return pltpu.make_async_copy(wx_ref.at[:, cols], wx.at[j], w_s.at[4 + j])

    def rows_of(r):
        return pl.ds(pl.multiple_of(r * step, step), step)

    def send(kind, src, dst, r, dev):
        return pltpu.make_async_remote_copy(src_ref=src, dst_ref=dst.at[r], send_sem=send_s.at[kind, r],
                                            recv_sem=rec_s.at[kind, r], device_id={"tensor": dev},
                                            device_id_type=MESH)

    def c_att(r):
        return send(0, a_ref.at[rows_of(r), :], am, r, mate)

    def c_part(r):
        return send(1, ps.at[r], pm, r, mate)

    def c_fo(r):
        return send(2, tfo.at[r], sfo, r, peer)

    def c_pe(r):
        return send(3, tpe.at[r], spe, r, peer)

    def c_fin(r):
        return send(4, fs.at[r], f, r, mate)

    def dot(lhs, rhs):
        return jnp.dot(lhs, rhs, preferred_element_type=jnp.float32)

    def mine(r):
        return a_ref[rows_of(r), :]

    def each(fn):
        def one(r, _):
            fn(r)
            return 0

        lax.fori_loop(0, chunks, one, 0)

    def store(r, total):
        o_ref[rows_of(r), :] = (
            res_ref[rows_of(r), :].astype(jnp.float32) + gate_ref[...][None, :] * total
        ).astype(o_ref.dtype)

    barrier = pltpu.get_barrier_semaphore()
    pl.semaphore_signal(barrier, inc=1, device_id={"tensor": mate}, device_id_type=MESH)

    @pl.when(inner)
    def _():
        pl.semaphore_signal(barrier, inc=1, device_id={"tensor": peer}, device_id_type=MESH)
        pl.semaphore_wait(barrier, 2)
        order = (load(far + jfo), load_x(jfo), load(far + jpe), load_x(jpe), load(mate), load(z))
        for copy in order:
            copy.start()
        for copy in order[:2]:
            copy.wait()

        @each
        def _(r):
            c_att(r).wait_recv()
            tfo[r] = (dot(mine(r), w[far + jfo]) + dot(am[r], wx[jfo])).astype(jnp.bfloat16)
            c_fo(r).start()

        for copy in order[2:]:
            copy.wait()

        @each
        def _(r):
            tpe[r] = (dot(mine(r), w[far + jpe]) + dot(am[r], wx[jpe])).astype(jnp.bfloat16)
            c_pe(r).start()
            own_s[r] = dot(mine(r), w[mate])
            c_fo(r).wait_recv()
            fs[r] = (own_s[r] + sfo[r].astype(jnp.float32)).astype(jnp.bfloat16)
            c_fin(r).start()

        @each
        def _(r):
            own_s[r] = dot(mine(r), w[z])

        @each
        def _(r):
            c_part(r).wait_recv()
            c_pe(r).wait_recv()
            store(r, own_s[r] + pm[r].astype(jnp.float32) + spe[r].astype(jnp.float32))

        @each
        def _(r):
            c_fo(r).wait_send()
            c_pe(r).wait_send()
            c_fin(r).wait_send()

    @pl.when(outer)
    def _():
        pl.semaphore_wait(barrier, 1)

        @each
        def _(r):
            c_att(r).start()

        order = (load(mate), load(z))
        for copy in order:
            copy.start()
        for copy in order:
            copy.wait()

        @each
        def _(r):
            ps[r] = dot(mine(r), w[mate]).astype(jnp.bfloat16)
            c_part(r).start()
            own_s[r] = dot(mine(r), w[z])

        @each
        def _(r):
            c_fin(r).wait_recv()
            store(r, own_s[r] + f[r].astype(jnp.float32))

        @each
        def _(r):
            c_att(r).wait_send()
            c_part(r).wait_send()


def line_project(attended, weight_mate, out_weight, residual, gate):
    rows, cols = attended.shape
    share = out_weight.shape[1] // 4
    chunks = rows // 128
    vmem = pl.BlockSpec(memory_space=pltpu.VMEM)
    hbm = pl.BlockSpec(memory_space=pl.ANY)
    dma = pltpu.SemaphoreType.DMA
    bf16, f32 = jnp.bfloat16, jnp.float32
    blocks = [pltpu.VMEM((chunks, 128, share), bf16) for _ in range(7)]
    return pl.pallas_call(
        project_kernel,
        in_specs=[vmem, hbm, hbm, vmem, vmem],
        out_specs=vmem,
        out_shape=jax.ShapeDtypeStruct((rows, share), bf16),
        scratch_shapes=[
            pltpu.VMEM((4, cols, share), bf16),
            pltpu.VMEM((2, cols, share), bf16),
            pltpu.VMEM((chunks, 128, cols), bf16),
            *blocks,
            pltpu.VMEM((chunks, 128, share), bf16),
            pltpu.VMEM((chunks, 128, share), f32),
            dma((6,)),
            dma((5, chunks)),
            dma((5, chunks)),
        ],
        compiler_params=pltpu.CompilerParams(
            collective_id=2, has_side_effects=True, vmem_limit_bytes=56 * 2**20
        ),
        name="line_project",
    )(attended, out_weight, weight_mate, residual, gate)


def general_body(n, query, key_fresh, value_fresh, key_stale, value_stale, out_weight, residual, gate):
    rows, cols = query.shape
    if n == 8 and lax.axis_size("tensor") == 4 and cols % (2 * HD) == 0:
        attended, weight_mate = paired_attention(
            query, key_fresh, value_fresh, key_stale, value_stale, out_weight
        )
        return line_project(attended, weight_mate, out_weight, residual, gate)
    keys = lax.all_gather(key_stale, "patch", axis=0, tiled=True)
    values = lax.all_gather(value_stale, "patch", axis=0, tiled=True)
    local = pl.BlockSpec((rows, HD), lambda h: (0, h))
    whole = pl.BlockSpec((rows * n, HD), lambda h: (0, h))
    attended = pl.pallas_call(
        functools.partial(flash_kernel, n),
        grid=(cols // HD,),
        in_specs=[local, local, local, whole, whole],
        out_specs=local,
        out_shape=jax.ShapeDtypeStruct((rows, cols), jnp.bfloat16),
        compiler_params=pltpu.CompilerParams(vmem_limit_bytes=48 * 2**20),
        name="flash",
    )(query, key_fresh, value_fresh, keys, values)
    return project(attended, out_weight, residual, gate)


def project(attended, out_weight, residual, gate):
    partial = jnp.dot(attended, out_weight, preferred_element_type=jnp.float32).astype(jnp.bfloat16)
    mine = lax.psum_scatter(partial, "tensor", scatter_dimension=1, tiled=True).astype(jnp.float32)
    return (residual.astype(jnp.float32) + gate[None, :] * mine).astype(jnp.bfloat16)


def solution(mesh):
    n = mesh.shape["patch"]
    both = P("patch", "tensor")
    return jax.shard_map(
        functools.partial(general_body, n),
        mesh=mesh,
        in_specs=(both,) * 5 + (P("tensor", None), both, P("tensor")),
        out_specs=both,
        check_vma=False,
    )
```
